32 devices in a mesh: member: 2 (over y), face: 4 (over z), slot: 2 (over x), chan: 2 (over core).
Axes of the slice: x: 2, y: 2, z: 4, core: 2. Of those that a mesh axis runs over, the one named last changes fastest.
Arguments:
- observed: bfloat16 [16384, 128], P(('member', 'face', 'slot')), parts along dimension 0, may hold values from -6 to 6
- target_face: int32 [16384, 1], P(('member', 'face', 'slot')), parts along dimension 0, may hold values from 0 to 3; in each aligned block of 1024 rows (0 to 1023, 1024 to 2047, ...) at most 512 rows name the same one
- target_cell: int32 [16384], P(('member', 'face', 'slot')), parts along dimension 0, may hold values from 0 to 319
- node_embed: bfloat16 [1280, 1024], P(('face', 'slot'), 'chan'), may hold values from -6 to 6
- neighbours: int32 [6, 1280], P(None, ('face', 'slot')), may hold values from 0 to 223, as said below
- edge_weight: float32 [6, 1280], P(None, ('face', 'slot')), may hold values from 0.05 to 0.35
- w_embed: bfloat16 [128, 1024], replicated, may hold values from -0.5 to 0.5
- w_key: bfloat16 [1024, 1024], P(None, 'chan'), may hold values from -0.1875 to 0.1875
- w_mix: bfloat16 [1024, 1024], P(None, 'chan'), may hold values from -0.1875 to 0.1875
- w_back: bfloat16 [1024, 1024], P('chan'), may hold values from -0.1875 to 0.1875
- w_out: bfloat16 [1024, 128], P('chan'), may hold values from -0.1875 to 0.1875
Outputs:
- predicted: bfloat16 [16384, 128], P(('member', 'face', 'slot')), parts along dimension 0
- state: bfloat16 [2560, 1024], P(('member', 'face', 'slot'), 'chan'), parts along dimension 0
The draws below stay inside these ranges and needn't reach their ends.
There are 2 independent parts, one for each index of `member`. The reference program is written for one: setup_inputs(seed, part) draws one part's arguments, and reference() takes and returns one part's arrays. A program takes and returns all parts, laid end to end along the dimension named above; an argument that names none is the same for every part. Nothing has to cross between parts.
Inputs may be any that keep to these rules, and one draw needn't show every extreme that they name: `target_face`: within the rows of one device (1024) no face region is named by more than 512 rows, and in some device one face region is named by exactly 512 rows. `neighbours`: entry [j, n] lies within 32 positions of n's own position, which is (n mod 160) + 32.
All inputs are finite; a program needn't handle non-finite values.
Results may differ from the reference program's by a relative error of at most 0.014.
Values may be sent and summed in bfloat16 or wider, within the bound.
A program may use at most 64 MiB of HBM per device.

```python
import math
import jax
import jax.numpy as jnp
import numpy as np
from jax import lax

F = 128
C = 1024
HD = 64
K = 6
HALO = 32
ROW_DEV = 1024
NODE_ROWS = 160
ROWS = 8192
NODES = 1280
CAP = 512
N_FACE = 4
N_SLOT = 2


def draw_neighbours(key, part):
    key = jax.random.fold_in(key, 7)
    offsets = jax.random.randint(key, (K, NODES), -HALO, HALO + 1)
    offsets = offsets.at[0, 0].set(-HALO).at[0, NODES - 1].set(HALO)
    position = jnp.arange(NODES, dtype=jnp.int32) % NODE_ROWS
    return (position[None, :] + HALO + offsets).astype(jnp.int32)


def set_ends(entries, key, smallest, largest):
    place = [jax.random.randint(jax.random.fold_in(key, axis), (), 0, length) for axis, length in enumerate(entries.shape)]
    longest = entries.shape.index(max(entries.shape))
    next_to = place[:longest] + [(place[longest] + 1) % entries.shape[longest]] + place[longest + 1:]
    return entries.at[tuple(place)].set(smallest).at[tuple(next_to)].set(largest)


def shard_levels(own_key, shape, split, low, top_value):
    factor_of = 1.0
    for dim, parts in split:
        draws = jax.random.uniform(jax.random.fold_in(jax.random.fold_in(own_key, 6), dim), (parts,), jnp.float32, low / len(split), top_value / len(split))
        factor_of = factor_of * jnp.repeat(jnp.exp(draws), shape[dim] // parts).reshape((-1,) + (1,) * (len(shape) - 1 - dim))
    return factor_of


def shared_out(rng, own, number, rows, amount, top, bound, lean):
    ranking = jax.random.permutation(rng, amount)
    heavy_load, common = portions_of(amount, rows * top, bound, lean, True), portions_of(amount, rows * top, bound, lean, False)
    places = jnp.arange(amount)

    def named(lengths, turn):
        used = int((lengths > 0).sum())
        fixed = max(1, used // 4)
        passed = fixed + (places - fixed + turn * (used - fixed)) % max(1, amount - fixed)
        return jnp.zeros((amount,), jnp.int32).at[ranking[jnp.where(places < fixed, places, passed)]].set(jnp.asarray(lengths, jnp.int32))

    lengths = jnp.where(number % 4 == 0, named(heavy_load, number // 4), named(common, number - number // 4 - 1))
    mixed = jax.random.permutation(jax.random.fold_in(own, 3), amount)
    giver, receiver = mixed[0:amount // 2 * 2:2], mixed[1:amount // 2 * 2:2]
    room = jnp.minimum(lengths[giver] - 1, bound - lengths[receiver]) // 2
    room = jnp.where((giver == ranking[0]) | (receiver == ranking[0]) | (lengths[receiver] == 0), 0, jnp.maximum(room, 0))
    passed = jax.random.randint(jax.random.fold_in(own, 4), (amount // 2,), 0, 1 << 20) % (room + 1)
    lengths = lengths.at[giver].add(-passed).at[receiver].add(passed)
    items = jnp.searchsorted(jnp.cumsum(lengths), jnp.arange(rows * top), side="right").astype(jnp.int32)
    listing = items.reshape(top, rows).T
    listing = listing[jax.random.permutation(jax.random.fold_in(own, 1), rows)]
    turn = jax.random.randint(jax.random.fold_in(own, 2), (rows, 1), 0, top)
    return jnp.take_along_axis(listing, (jnp.arange(top)[None, :] + turn) % top, axis=1)


def portions_of(number_of, total, bound, skew, full):
    portions = [(1 << 20) // math.isqrt(rank ** skew) + 1 for rank in range(1, number_of + 1)]
    largest = bound if full else min(bound, max(-(-total // number_of), total * portions[0] // sum(portions)))
    least = 1 if total - largest >= number_of - 1 else 0
    holding, surplus = [largest] + [least] * (number_of - 1), total - largest - least * (number_of - 1)
    while surplus > 0:
        candidates = [i for i in range(1, number_of) if holding[i] < largest] or [i for i in range(1, number_of) if holding[i] < bound]
        pool, remaining = sum([portions[i] for i in candidates]), surplus
        for i in candidates:
            more = min(bound - holding[i], max(1, remaining * portions[i] // pool), surplus)
            holding[i] = holding[i] + more
            surplus = surplus - more
    return np.array(holding)


def scatter_about(rng, extent, spread, reach, shards=(), kind=jnp.bfloat16):
    factor_of = shard_levels(rng, extent, shards, -0.22, 0.18) if shards else 1.0
    entries = jax.random.normal(rng, extent, jnp.float32) * spread * factor_of
    return jnp.minimum(jnp.maximum(entries, -reach), reach).astype(kind)


def setup_inputs(seed: int = 0, part: int = 0) -> dict:
    key_of = jax.random.split(jax.random.key(seed), 12)
    part_splits = jax.random.split(jax.random.fold_in(key_of[11], part), 12)
    observed = scatter_about(part_splits[0], (ROWS, F), 1.0, 6.0, ((0, 8),))
    target_face_keys = jax.random.split(jax.random.fold_in(part_splits[1], 1), ROWS // ROW_DEV)
    target_face_turns = jax.random.permutation(jax.random.fold_in(part_splits[1], 3), ROWS // ROW_DEV)
    target_face = jax.vmap(lambda own, number: shared_out(jax.random.fold_in(part_splits[1], 2), own, number, ROW_DEV, N_FACE, 1, CAP, 2))(target_face_keys, target_face_turns).reshape((ROWS, 1))
    target_cell = set_ends(jax.random.randint(part_splits[2], (ROWS,), 0, NODE_ROWS * N_SLOT), jax.random.fold_in(part_splits[2], 1), 0, (NODE_ROWS * N_SLOT) - 1).astype(jnp.int32)
    node_embed = scatter_about(key_of[3], (NODES, C), 1.0, 6.0, ((0, 8), (1, 2)))
    neighbours = draw_neighbours(jax.random.fold_in(key_of[11], 71), part)
    edge_weight = jnp.clip(jnp.exp(math.log(0.35) - 1.9459101 * jax.random.uniform(key_of[5], (K, NODES), jnp.float32) ** shard_levels(key_of[5], (K, NODES), ((1, 8),), -0.2, 0.2)), 0.05, 0.35)
    w_embed = scatter_about(key_of[6], (F, C), F ** -0.5, 0.5)
    w_key = scatter_about(key_of[7], (C, C), C ** -0.5, 0.1875, ((1, 2),))
    w_mix = scatter_about(key_of[8], (C, C), C ** -0.5, 0.1875, ((1, 2),))
    w_back = scatter_about(key_of[9], (C, C), C ** -0.5, 0.1875, ((0, 2),))
    w_out = scatter_about(key_of[10], (C, F), C ** -0.5, 0.1875, ((0, 2),))
    return dict(observed=observed, target_face=target_face, target_cell=target_cell, node_embed=node_embed, neighbours=neighbours, edge_weight=edge_weight, w_embed=w_embed, w_key=w_key, w_mix=w_mix, w_back=w_back, w_out=w_out)


def reference(observed, target_face, target_cell, node_embed, neighbours, edge_weight, w_embed, w_key, w_mix, w_back, w_out):
    per_face = NODE_ROWS * N_SLOT
    node = (target_face[:, 0] * per_face + target_cell).astype(jnp.int32)
    embedded = jax.nn.gelu(jnp.dot(observed, w_embed, preferred_element_type=jnp.float32)).astype(jnp.bfloat16)
    keys = jnp.dot(embedded, w_key, preferred_element_type=jnp.float32).astype(jnp.bfloat16)
    picked = node_embed[node]
    heads = C // HD
    score = lax.optimization_barrier(jnp.sum((picked.astype(jnp.float32) * keys.astype(jnp.float32)).reshape(-1, heads, HD), axis=2)) / math.sqrt(HD)
    attend = jax.nn.sigmoid(score)
    contrib = jnp.repeat(attend, HD, axis=1) * embedded.astype(jnp.float32)
    numer = jax.ops.segment_sum(contrib, node, NODES)
    denom = jax.ops.segment_sum(attend, node, NODES)
    latent = (node_embed.astype(jnp.float32) + numer / (1.0 + jnp.repeat(denom, HD, axis=1))).astype(jnp.bfloat16)
    nodes = jnp.arange(NODES, dtype=jnp.int32)
    source = (nodes[None, :] + neighbours - HALO - (nodes % NODE_ROWS)[None, :]) % NODES
    summed = lax.optimization_barrier(jnp.sum(edge_weight[:, :, None] * latent[source].astype(jnp.float32), axis=0)).astype(jnp.bfloat16)
    hidden = jax.nn.gelu(jnp.dot(summed, w_mix, preferred_element_type=jnp.float32)).astype(jnp.bfloat16)
    state = (latent.astype(jnp.float32) + jnp.dot(hidden, w_back, preferred_element_type=jnp.float32)).astype(jnp.bfloat16)
    predicted = jnp.dot(state[node], w_out, preferred_element_type=jnp.float32).astype(jnp.bfloat16)
    return (predicted, state)
```

```python
import functools

import jax
import jax.numpy as jnp
from jax import lax
from jax.experimental import pallas as pl
from jax.experimental.pallas import tpu as pltpu
from jax.sharding import PartitionSpec as P

HD = 64
HALO = 32
LANES = 128
MESH = pl.DeviceIdType.MESH
F32 = jnp.float32
BF16 = jnp.bfloat16


def dot(a, b):
    return jnp.dot(a, b, preferred_element_type=F32)


def dot_tn(a, b):
    return lax.dot_general(a, b, (((0,), (0,)), ((), ())), preferred_element_type=F32)


def dot_nt(a, b):
    return lax.dot_general(a, b, (((1,), (1,)), ((), ())), preferred_element_type=F32)


def ones_where(mask):
    return jnp.where(mask, 1.0, 0.0).astype(BF16)


def two_parts(x):
    high = x.astype(BF16)
    return high, (x - high.astype(F32)).astype(BF16)


def kernel(
    faces,
    slots,
    observed,
    face_row,
    cell_row,
    node_col,
    node_embed,
    neighbours,
    edge_weight,
    w_embed,
    w_key,
    w_mix,
    w_back,
    w_out,
    predicted,
    state_out,
    rows_out,
    rows_in,
    cells_out,
    cells_in,
    queries,
    embedded,
    numer,
    denom,
    sums_out,
    sums_in,
    wide,
    mix_parts,
    back_out,
    back_in,
    part_out,
    part_in,
    table,
    row_sem,
    cell_sem,
    query_sem,
    sums_sem,
    halo_sem,
    chan_sem,
    table_sem,
):
    row_count = observed.shape[0]
    cap = rows_in.shape[1]
    nodes, width = node_embed.shape
    blocks = faces * slots
    face_nodes = slots * nodes
    face, slot, chan = lax.axis_index("face"), lax.axis_index("slot"), lax.axis_index("chan")
    block = face * slots + slot
    other = 1 - chan

    def block_id(index):
        return {"face": index // slots, "slot": lax.rem(index, slots)}

    barrier = pltpu.get_barrier_semaphore()

    def greet(k, carry):
        pl.semaphore_signal(
            barrier, inc=1, device_id=block_id(lax.rem(block + k, blocks)), device_id_type=MESH
        )
        return carry

    lax.fori_loop(1, blocks, greet, 0)
    pl.semaphore_signal(barrier, inc=1, device_id={"chan": other}, device_id_type=MESH)

    face_of = face_row[...]
    sub = lax.broadcasted_iota(jnp.int32, (max(8, faces), row_count), 0)
    lane = lax.broadcasted_iota(jnp.int32, (max(8, faces), row_count), 1)
    aimed = jnp.where(sub == face_of, 1, 0)
    count = aimed
    step = 1
    while step < row_count:
        count = count + jnp.where(lane >= step, pltpu.roll(count, step, 1), 0)
        step *= 2
    place = jnp.sum(aimed * (count - 1), axis=0, keepdims=True) + face_of * cap
    cell1 = cell_row[...] + 1
    sub16 = lax.broadcasted_iota(jnp.int32, (16, row_count), 0)
    cell_parts = (
        jnp.where(sub16 == 0, cell1 >> 7, jnp.where(sub16 == 1, cell1 & 127, 0))
        .astype(F32)
        .astype(BF16)
    )

    def bucket(goal):
        pick = ones_where(
            lax.broadcasted_iota(jnp.int32, (cap, row_count), 0) == place - goal * cap
        )
        parts = dot_nt(cell_parts, pick)
        cells = (parts[0:1] * 128.0 + parts[1:2]).astype(jnp.int32) - 1
        return dot(pick, observed[...]).astype(BF16), jnp.broadcast_to(cells, (8, cap))

    rows, cells = bucket(face)
    rows_in[0] = rows
    cells_in[0] = cells
    queries[pl.ds(slot * nodes, nodes)] = node_embed[...]

    pl.semaphore_wait(barrier, blocks)

    def query_copy(k):
        mine = queries.at[pl.ds(slot * nodes, nodes)]
        return pltpu.make_async_remote_copy(
            src_ref=node_embed,
            dst_ref=mine,
            send_sem=query_sem.at[0, k],
            recv_sem=query_sem.at[1, k],
            device_id={"slot": lax.rem(slot + k, slots)},
            device_id_type=MESH,
        )

    for k in range(1, slots):
        query_copy(k).start()

    def row_copy(k):
        return pltpu.make_async_remote_copy(
            src_ref=rows_out.at[k],
            dst_ref=rows_in.at[k],
            send_sem=row_sem.at[0, k],
            recv_sem=row_sem.at[1, k],
            device_id={"face": lax.rem(face + k, faces)},
            device_id_type=MESH,
        )

    def cell_copy(k):
        return pltpu.make_async_remote_copy(
            src_ref=cells_out.at[k],
            dst_ref=cells_in.at[k],
            send_sem=cell_sem.at[0, k],
            recv_sem=cell_sem.at[1, k],
            device_id={"face": lax.rem(face + k, faces)},
            device_id_type=MESH,
        )

    def send_rows(k, carry):
        rows, cells = bucket(lax.rem(face + k, faces))
        rows_out[k] = rows
        cells_out[k] = cells
        row_copy(k).start()
        cell_copy(k).start()
        return carry

    lax.fori_loop(1, faces, send_rows, 0)

    group = ones_where(
        lax.broadcasted_iota(jnp.int32, (width, LANES), 0) // HD
        == lax.broadcasted_iota(jnp.int32, (width, LANES), 1)
    )
    spread = ones_where(
        lax.broadcasted_iota(jnp.int32, (LANES, width), 1) // HD
        == lax.broadcasted_iota(jnp.int32, (LANES, width), 0)
    )
    numer[...] = jnp.zeros_like(numer)
    denom[...] = jnp.zeros_like(denom)

    for k in range(1, slots):
        query_copy(k).wait()

    def attend_block(k, carry):
        @pl.when(k > 0)
        def _():
            row_copy(k).wait()
            cell_copy(k).wait()

        x = rows_in[k]
        chunk = 256
        for j in range(0, w_embed.shape[1], chunk):
            embedded[:, j : j + chunk] = jax.nn.gelu(dot(x, w_embed[:, j : j + chunk])).astype(BF16)
        keys = dot(embedded[...], w_key[...]).astype(BF16).astype(F32)
        hit = ones_where(
            lax.broadcasted_iota(jnp.int32, (face_nodes, cap), 0) == cells_in[k][0:1]
        )
        picked = dot_tn(hit, queries[...])
        score = dot((picked * keys).astype(BF16), group) * (HD**-0.5)
        attend = jax.nn.sigmoid(score).astype(BF16)
        values = embedded[:, pl.ds(pl.multiple_of(chan * width, width), width)]
        contrib = (dot(attend, spread) * values.astype(F32)).astype(BF16)
        numer[...] += dot(hit, contrib)
        denom[...] += dot(hit, attend)
        return carry

    lax.fori_loop(0, faces, attend_block, 0)

    def sums_copy(k):
        return pltpu.make_async_remote_copy(
            src_ref=sums_out.at[k],
            dst_ref=sums_in.at[k],
            send_sem=sums_sem.at[0, k],
            recv_sem=sums_sem.at[1, k],
            device_id={"slot": lax.rem(slot + k, slots)},
            device_id_type=MESH,
        )

    for k in range(1, slots):
        theirs = pl.ds(lax.rem(slot + k, slots) * nodes, nodes)
        sums_out[k, :, :width] = numer[theirs].astype(BF16)
        sums_out[k, :, width:] = denom[theirs].astype(BF16)
        sums_copy(k).start()

    extended = nodes + 2 * HALO
    position = lax.broadcasted_iota(jnp.int32, (extended, nodes), 0)
    weights = jnp.zeros((extended, nodes), F32)
    for j in range(neighbours.shape[0]):
        weights += jnp.where(position == neighbours[j : j + 1], edge_weight[j : j + 1], 0.0)
    weights_high, weights_low = two_parts(weights)

    mine = pl.ds(slot * nodes, nodes)
    total = numer[mine]
    weight = denom[mine]
    for k in range(1, slots):
        sums_copy(k).wait()
        total += sums_in[k, :, :width].astype(F32)
        weight += sums_in[k, :, width:].astype(F32)
    weight_high, weight_low = two_parts(weight)
    weight = dot(weight_high, spread) + dot(weight_low, spread)
    latent = (node_embed[...].astype(F32) + total / (1.0 + weight)).astype(BF16)
    wide[HALO : HALO + nodes] = latent

    right = pltpu.make_async_remote_copy(
        src_ref=wide.at[pl.ds(nodes, HALO)],
        dst_ref=wide.at[pl.ds(0, HALO)],
        send_sem=halo_sem.at[0, 0],
        recv_sem=halo_sem.at[1, 0],
        device_id=block_id(lax.rem(block + 1, blocks)),
        device_id_type=MESH,
    )
    left = pltpu.make_async_remote_copy(
        src_ref=wide.at[pl.ds(HALO, HALO)],
        dst_ref=wide.at[pl.ds(HALO + nodes, HALO)],
        send_sem=halo_sem.at[0, 1],
        recv_sem=halo_sem.at[1, 1],
        device_id=block_id(lax.rem(block + blocks - 1, blocks)),
        device_id_type=MESH,
    )
    right.start()
    left.start()
    right.wait()
    left.wait()

    def chan_copy(k, source, goal):
        return pltpu.make_async_remote_copy(
            src_ref=source,
            dst_ref=goal,
            send_sem=chan_sem.at[0, k],
            recv_sem=chan_sem.at[1, k],
            device_id={"chan": other},
            device_id_type=MESH,
        )

    around = wide[...]
    summed = (dot_tn(weights_high, around) + dot_tn(weights_low, around)).astype(BF16)
    mix_parts[0] = summed
    mix_copy = chan_copy(0, mix_parts.at[0], mix_parts.at[1])
    mix_copy.start()
    mixed = dot(summed, w_mix[pl.ds(pl.multiple_of(chan * width, width), width)])
    mix_copy.wait()
    mixed += dot(mix_parts[1], w_mix[pl.ds(pl.multiple_of(other * width, width), width)])
    hidden = jax.nn.gelu(mixed).astype(BF16)
    back_out[...] = dot(
        hidden, w_back[:, pl.ds(pl.multiple_of(other * width, width), width)]
    ).astype(BF16)
    back_copy = chan_copy(1, back_out, back_in)
    back_copy.start()
    update = dot(hidden, w_back[:, pl.ds(pl.multiple_of(chan * width, width), width)])
    back_copy.wait()
    state = (latent.astype(F32) + update + back_in[...].astype(F32)).astype(BF16)
    state_out[...] = state

    part = dot(state, w_out[...])
    part_out[...] = part
    part_copy = chan_copy(2, part_out, part_in)
    part_copy.start()
    part_copy.wait()
    here = pl.ds(block * nodes, nodes)
    table[here] = (part + part_in[...]).astype(BF16)

    def table_copy(k):
        return pltpu.make_async_remote_copy(
            src_ref=table.at[here],
            dst_ref=table.at[here],
            send_sem=table_sem.at[0, k],
            recv_sem=table_sem.at[1, k],
            device_id=block_id(lax.rem(block + k, blocks)),
            device_id_type=MESH,
        )

    def send_table(k, carry):
        table_copy(k).start()
        return carry

    lax.fori_loop(1, blocks, send_table, 0)
    node_of = node_col[...]

    def decode(k, total):
        source = lax.rem(block + blocks - k, blocks)

        @pl.when(k > 0)
        def _():
            table_copy(k).wait()

        hit = ones_where(
            lax.broadcasted_iota(jnp.int32, (row_count, nodes), 1) == node_of - source * nodes
        )
        return total + dot(hit, table[pl.ds(source * nodes, nodes)])

    total = lax.fori_loop(0, blocks, decode, jnp.zeros(predicted.shape, F32))
    predicted[...] = total.astype(BF16)


def body(
    observed,
    target_face,
    target_cell,
    node_embed,
    neighbours,
    edge_weight,
    w_embed,
    w_key,
    w_mix,
    w_back,
    w_out,
):
    faces, slots = lax.axis_size("face"), lax.axis_size("slot")
    row_count, features = observed.shape
    nodes, width = node_embed.shape
    channels = w_embed.shape[1]
    cap = 2 * row_count // faces
    blocks = faces * slots
    face_row = target_face.reshape(1, row_count)
    cell_row = target_cell.reshape(1, row_count)
    node_col = target_face * (nodes * slots) + target_cell[:, None]
    vmem = pl.BlockSpec(memory_space=pltpu.VMEM)
    dma = pltpu.SemaphoreType.DMA
    return pl.pallas_call(
        functools.partial(kernel, faces, slots),
        out_shape=(
            jax.ShapeDtypeStruct((row_count, w_out.shape[1]), BF16),
            jax.ShapeDtypeStruct((nodes, width), BF16),
        ),
        in_specs=[vmem] * 12,
        out_specs=(vmem, vmem),
        scratch_shapes=[
            pltpu.VMEM((faces, cap, features), BF16),
            pltpu.VMEM((faces, cap, features), BF16),
            pltpu.VMEM((faces, 8, cap), jnp.int32),
            pltpu.VMEM((faces, 8, cap), jnp.int32),
            pltpu.VMEM((slots * nodes, width), BF16),
            pltpu.VMEM((cap, channels), BF16),
            pltpu.VMEM((slots * nodes, width), F32),
            pltpu.VMEM((slots * nodes, LANES), F32),
            pltpu.VMEM((slots, nodes, width + LANES), BF16),
            pltpu.VMEM((slots, nodes, width + LANES), BF16),
            pltpu.VMEM((nodes + 2 * HALO, width), BF16),
            pltpu.VMEM((2, nodes, width), BF16),
            pltpu.VMEM((nodes, width), BF16),
            pltpu.VMEM((nodes, width), BF16),
            pltpu.VMEM((nodes, w_out.shape[1]), F32),
            pltpu.VMEM((nodes, w_out.shape[1]), F32),
            pltpu.VMEM((blocks * nodes, w_out.shape[1]), BF16),
            dma((2, faces)),
            dma((2, faces)),
            dma((2, slots)),
            dma((2, slots)),
            dma((2, 2)),
            dma((2, 3)),
            dma((2, blocks)),
        ],
        compiler_params=pltpu.CompilerParams(
            collective_id=0, has_side_effects=True, vmem_limit_bytes=48 * 1024 * 1024
        ),
    )(
        observed,
        face_row,
        cell_row,
        node_col,
        node_embed,
        neighbours,
        edge_weight,
        w_embed,
        w_key,
        w_mix,
        w_back,
        w_out,
    )


def solution(mesh):
    in_specs = (
        P(("member", "face", "slot"), None),
        P(("member", "face", "slot"), None),
        P(("member", "face", "slot")),
        P(("face", "slot"), "chan"),
        P(None, ("face", "slot")),
        P(None, ("face", "slot")),
        P(),
        P(None, "chan"),
        P(None, "chan"),
        P("chan", None),
        P("chan", None),
    )
    out_specs = (P(("member", "face", "slot"), None), P(("member", "face", "slot"), "chan"))
    return jax.shard_map(body, mesh=mesh, in_specs=in_specs, out_specs=out_specs, check_vma=False)
```

```python
import functools

import jax
import jax.numpy as jnp
from jax import lax
from jax.experimental import pallas as pl
from jax.experimental.pallas import tpu as pltpu
from jax.sharding import PartitionSpec as P

HD = 64
HALO = 32
LANES = 128
INPUTS = 11
MESH = pl.DeviceIdType.MESH
F32 = jnp.float32
BF16 = jnp.bfloat16


def dot(a, b):
    return jnp.dot(a, b, preferred_element_type=F32)


def dot_tn(a, b):
    return lax.dot_general(a, b, (((0,), (0,)), ((), ())), preferred_element_type=F32)


def dot_nt(a, b):
    return lax.dot_general(a, b, (((1,), (1,)), ((), ())), preferred_element_type=F32)


def ones_where(mask):
    return jnp.where(mask, 1.0, 0.0).astype(BF16)


def two_parts(x):
    high = x.astype(BF16)
    return high, (x - high.astype(F32)).astype(BF16)


def kernel(
    faces,
    slots,
    *refs,
):
    arrays, refs = refs[:INPUTS], refs[INPUTS:]
    predicted, state_out = refs[:2]
    held, refs = refs[2 : 2 + INPUTS], refs[2 + INPUTS :]
    (
        load_sem,
        rows_out,
        rows_in,
        cells_out,
        cells_in,
        queries,
        embedded,
        numer,
        denom,
        sums_out,
        sums_in,
        wide,
        mix_parts,
        back_out,
        back_in,
        part_out,
        part_in,
        table,
        chosen,
        row_sem,
        cell_sem,
        query_sem,
        sums_sem,
        halo_sem,
        chan_sem,
        table_sem,
    ) = refs
    loads = [
        pltpu.make_async_copy(array, into, load_sem.at[i])
        for i, (array, into) in enumerate(zip(arrays, held))
    ]
    for load in loads:
        load.start()
    (
        face_row,
        cell_row,
        observed,
        node_embed,
        w_embed,
        w_key,
        neighbours,
        edge_weight,
        w_mix,
        w_back,
        w_out,
    ) = held
    row_count = observed.shape[0]
    cap = rows_in.shape[1]
    nodes, width = node_embed.shape
    blocks = faces * slots
    face_nodes = slots * nodes
    face, slot, chan = lax.axis_index("face"), lax.axis_index("slot"), lax.axis_index("chan")
    block = face * slots + slot
    other = 1 - chan

    def block_id(index):
        return {"face": index // slots, "slot": lax.rem(index, slots)}

    barrier = pltpu.get_barrier_semaphore()

    def greet(k, carry):
        pl.semaphore_signal(
            barrier, inc=1, device_id=block_id(lax.rem(block + k, blocks)), device_id_type=MESH
        )
        return carry

    lax.fori_loop(1, blocks, greet, 0)
    pl.semaphore_signal(barrier, inc=1, device_id={"chan": other}, device_id_type=MESH)

    for load in loads[:4]:
        load.wait()

    face_of = face_row[...]
    sub = lax.broadcasted_iota(jnp.int32, (max(8, faces), row_count), 0)
    lane = lax.broadcasted_iota(jnp.int32, (max(8, faces), row_count), 1)
    aimed = jnp.where(sub == face_of, 1, 0)
    count = aimed
    step = 1
    while step < row_count:
        count = count + jnp.where(lane >= step, pltpu.roll(count, step, 1), 0)
        step *= 2
    place = jnp.sum(aimed * (count - 1), axis=0, keepdims=True) + face_of * cap
    cell1 = cell_row[...] + 1
    sub16 = lax.broadcasted_iota(jnp.int32, (16, row_count), 0)
    cell_parts = (
        jnp.where(sub16 == 0, cell1 >> 7, jnp.where(sub16 == 1, cell1 & 127, 0))
        .astype(F32)
        .astype(BF16)
    )

    def bucket(goal):
        pick = ones_where(
            lax.broadcasted_iota(jnp.int32, (cap, row_count), 0) == place - goal * cap
        )
        parts = dot_nt(cell_parts, pick)
        cells = (parts[0:1] * 128.0 + parts[1:2]).astype(jnp.int32) - 1
        return dot(pick, observed[...]).astype(BF16), jnp.broadcast_to(cells, (8, cap))

    rows, cells = bucket(face)
    rows_in[0] = rows
    cells_in[0] = cells
    queries[pl.ds(slot * nodes, nodes)] = node_embed[...]

    pl.semaphore_wait(barrier, blocks)

    def query_copy(k):
        mine = queries.at[pl.ds(slot * nodes, nodes)]
        return pltpu.make_async_remote_copy(
            src_ref=node_embed,
            dst_ref=mine,
            send_sem=query_sem.at[0, k],
            recv_sem=query_sem.at[1, k],
            device_id={"slot": lax.rem(slot + k, slots)},
            device_id_type=MESH,
        )

    for k in range(1, slots):
        query_copy(k).start()

    def row_copy(k):
        return pltpu.make_async_remote_copy(
            src_ref=rows_out.at[k],
            dst_ref=rows_in.at[k],
            send_sem=row_sem.at[0, k],
            recv_sem=row_sem.at[1, k],
            device_id={"face": lax.rem(face + k, faces)},
            device_id_type=MESH,
        )

    def cell_copy(k):
        return pltpu.make_async_remote_copy(
            src_ref=cells_out.at[k],
            dst_ref=cells_in.at[k],
            send_sem=cell_sem.at[0, k],
            recv_sem=cell_sem.at[1, k],
            device_id={"face": lax.rem(face + k, faces)},
            device_id_type=MESH,
        )

    def send_rows(k, carry):
        rows, cells = bucket(lax.rem(face + k, faces))
        rows_out[k] = rows
        cells_out[k] = cells
        row_copy(k).start()
        cell_copy(k).start()
        return carry

    lax.fori_loop(1, faces, send_rows, 0)

    group = ones_where(
        lax.broadcasted_iota(jnp.int32, (width, LANES), 0) // HD
        == lax.broadcasted_iota(jnp.int32, (width, LANES), 1)
    )
    spread = ones_where(
        lax.broadcasted_iota(jnp.int32, (LANES, width), 1) // HD
        == lax.broadcasted_iota(jnp.int32, (LANES, width), 0)
    )
    numer[...] = jnp.zeros_like(numer)
    denom[...] = jnp.zeros_like(denom)

    node_of = jnp.broadcast_to(face_of * face_nodes + cell_row[...], (LANES, row_count)).T
    lane_of = lax.broadcasted_iota(jnp.int32, (row_count, LANES), 1)
    piece = chosen.shape[1]

    def choose(first):
        for j in range(0, piece, LANES):
            chosen[:, j : j + LANES] = ones_where(lane_of == node_of - (first + j))

    if piece == blocks * nodes:
        choose(0)
    for load in loads[4:6]:
        load.wait()
    for k in range(1, slots):
        query_copy(k).wait()

    def attend_block(k, carry):
        @pl.when(k > 0)
        def _():
            row_copy(k).wait()
            cell_copy(k).wait()

        x = rows_in[k]
        chunk = 256
        for j in range(0, w_embed.shape[1], chunk):
            embedded[:, j : j + chunk] = jax.nn.gelu(dot(x, w_embed[:, j : j + chunk])).astype(BF16)
        keys = dot(embedded[...], w_key[...]).astype(BF16).astype(F32)
        hit = ones_where(
            lax.broadcasted_iota(jnp.int32, (face_nodes, cap), 0) == cells_in[k][0:1]
        )
        picked = dot_tn(hit, queries[...])
        score = dot((picked * keys).astype(BF16), group) * (HD**-0.5)
        attend = jax.nn.sigmoid(score).astype(BF16)
        values = embedded[:, pl.ds(pl.multiple_of(chan * width, width), width)]
        contrib = (dot(attend, spread) * values.astype(F32)).astype(BF16)
        numer[...] += dot(hit, contrib)
        denom[...] += dot(hit, attend)
        return carry

    lax.fori_loop(0, faces, attend_block, 0)

    def sums_copy(k):
        return pltpu.make_async_remote_copy(
            src_ref=sums_out.at[k],
            dst_ref=sums_in.at[k],
            send_sem=sums_sem.at[0, k],
            recv_sem=sums_sem.at[1, k],
            device_id={"slot": lax.rem(slot + k, slots)},
            device_id_type=MESH,
        )

    for k in range(1, slots):
        theirs = pl.ds(lax.rem(slot + k, slots) * nodes, nodes)
        sums_out[k, :, :width] = numer[theirs].astype(BF16)
        sums_out[k, :, width:] = denom[theirs].astype(BF16)
        sums_copy(k).start()

    for load in loads[6:]:
        load.wait()

    extended = nodes + 2 * HALO
    position = lax.broadcasted_iota(jnp.int32, (extended, nodes), 0)
    weights = jnp.zeros((extended, nodes), F32)
    for j in range(neighbours.shape[0]):
        weights += jnp.where(position == neighbours[j : j + 1], edge_weight[j : j + 1], 0.0)
    weights_high, weights_low = two_parts(weights)

    mine = pl.ds(slot * nodes, nodes)
    total = numer[mine]
    weight = denom[mine]
    for k in range(1, slots):
        sums_copy(k).wait()
        total += sums_in[k, :, :width].astype(F32)
        weight += sums_in[k, :, width:].astype(F32)
    weight_high, weight_low = two_parts(weight)
    weight = dot(weight_high, spread) + dot(weight_low, spread)
    latent = (node_embed[...].astype(F32) + total / (1.0 + weight)).astype(BF16)
    wide[HALO : HALO + nodes] = latent

    right = pltpu.make_async_remote_copy(
        src_ref=wide.at[pl.ds(nodes, HALO)],
        dst_ref=wide.at[pl.ds(0, HALO)],
        send_sem=halo_sem.at[0, 0],
        recv_sem=halo_sem.at[1, 0],
        device_id=block_id(lax.rem(block + 1, blocks)),
        device_id_type=MESH,
    )
    left = pltpu.make_async_remote_copy(
        src_ref=wide.at[pl.ds(HALO, HALO)],
        dst_ref=wide.at[pl.ds(HALO + nodes, HALO)],
        send_sem=halo_sem.at[0, 1],
        recv_sem=halo_sem.at[1, 1],
        device_id=block_id(lax.rem(block + blocks - 1, blocks)),
        device_id_type=MESH,
    )
    right.start()
    left.start()
    right.wait()
    left.wait()

    def chan_copy(k, source, goal):
        return pltpu.make_async_remote_copy(
            src_ref=source,
            dst_ref=goal,
            send_sem=chan_sem.at[0, k],
            recv_sem=chan_sem.at[1, k],
            device_id={"chan": other},
            device_id_type=MESH,
        )

    around = wide[...]
    summed = (dot_tn(weights_high, around) + dot_tn(weights_low, around)).astype(BF16)
    mix_parts[0] = summed
    mix_copy = chan_copy(0, mix_parts.at[0], mix_parts.at[1])
    mix_copy.start()
    mixed = dot(summed, w_mix[pl.ds(pl.multiple_of(chan * width, width), width)])
    mix_copy.wait()
    mixed += dot(mix_parts[1], w_mix[pl.ds(pl.multiple_of(other * width, width), width)])
    hidden = jax.nn.gelu(mixed).astype(BF16)
    back_out[...] = dot(
        hidden, w_back[:, pl.ds(pl.multiple_of(other * width, width), width)]
    ).astype(BF16)
    back_copy = chan_copy(1, back_out, back_in)
    back_copy.start()
    update = dot(hidden, w_back[:, pl.ds(pl.multiple_of(chan * width, width), width)])
    back_copy.wait()
    state = (latent.astype(F32) + update + back_in[...].astype(F32)).astype(BF16)
    state_out[...] = state

    part = dot(state, w_out[...])
    part_out[...] = part
    part_copy = chan_copy(2, part_out, part_in)
    part_copy.start()
    part_copy.wait()
    here = pl.ds(block * nodes, nodes)
    table[here] = (part + part_in[...]).astype(BF16)

    def table_copy(k):
        return pltpu.make_async_remote_copy(
            src_ref=table.at[here],
            dst_ref=table.at[here],
            send_sem=table_sem.at[0, k],
            recv_sem=table_sem.at[1, k],
            device_id=block_id(lax.rem(block + k, blocks)),
            device_id_type=MESH,
        )

    def send_table(k, carry):
        table_copy(k).start()
        return carry

    lax.fori_loop(1, blocks, send_table, 0)

    def take_table(k, carry):
        table_copy(k).wait()
        return carry

    lax.fori_loop(1, blocks, take_table, 0)
    if piece == blocks * nodes:
        total = dot(chosen[...], table[...])
    else:

        def decode(k, total):
            choose(k * piece)
            return total + dot(chosen[...], table[pl.ds(k * piece, piece)])

        total = jnp.zeros(predicted.shape, F32)
        total = lax.fori_loop(0, blocks * nodes // piece, decode, total)
    predicted[...] = total.astype(BF16)


def body(
    observed,
    target_face,
    target_cell,
    node_embed,
    neighbours,
    edge_weight,
    w_embed,
    w_key,
    w_mix,
    w_back,
    w_out,
):
    faces, slots = lax.axis_size("face"), lax.axis_size("slot")
    row_count, features = observed.shape
    nodes, width = node_embed.shape
    channels = w_embed.shape[1]
    cap = 2 * row_count // faces
    blocks = faces * slots
    face_row = target_face.reshape(1, row_count)
    cell_row = target_cell.reshape(1, row_count)
    piece = blocks * nodes if blocks * nodes <= 4096 else slots * nodes
    arrays = (
        face_row,
        cell_row,
        observed,
        node_embed,
        w_embed,
        w_key,
        neighbours,
        edge_weight,
        w_mix,
        w_back,
        w_out,
    )
    vmem = pl.BlockSpec(memory_space=pltpu.VMEM)
    dma = pltpu.SemaphoreType.DMA
    return pl.pallas_call(
        functools.partial(kernel, faces, slots),
        out_shape=(
            jax.ShapeDtypeStruct((row_count, w_out.shape[1]), BF16),
            jax.ShapeDtypeStruct((nodes, width), BF16),
        ),
        in_specs=[pl.BlockSpec(memory_space=pl.ANY)] * INPUTS,
        out_specs=(vmem, vmem),
        scratch_shapes=[pltpu.VMEM(array.shape, array.dtype) for array in arrays]
        + [
            dma((INPUTS,)),
            pltpu.VMEM((faces, cap, features), BF16),
            pltpu.VMEM((faces, cap, features), BF16),
            pltpu.VMEM((faces, 8, cap), jnp.int32),
            pltpu.VMEM((faces, 8, cap), jnp.int32),
            pltpu.VMEM((slots * nodes, width), BF16),
            pltpu.VMEM((cap, channels), BF16),
            pltpu.VMEM((slots * nodes, width), F32),
            pltpu.VMEM((slots * nodes, LANES), F32),
            pltpu.VMEM((slots, nodes, width + LANES), BF16),
            pltpu.VMEM((slots, nodes, width + LANES), BF16),
            pltpu.VMEM((nodes + 2 * HALO, width), BF16),
            pltpu.VMEM((2, nodes, width), BF16),
            pltpu.VMEM((nodes, width), BF16),
            pltpu.VMEM((nodes, width), BF16),
            pltpu.VMEM((nodes, w_out.shape[1]), F32),
            pltpu.VMEM((nodes, w_out.shape[1]), F32),
            pltpu.VMEM((blocks * nodes, w_out.shape[1]), BF16),
            pltpu.VMEM((row_count, piece), BF16),
            dma((2, faces)),
            dma((2, faces)),
            dma((2, slots)),
            dma((2, slots)),
            dma((2, 2)),
            dma((2, 3)),
            dma((2, blocks)),
        ],
        compiler_params=pltpu.CompilerParams(
            collective_id=0, has_side_effects=True, vmem_limit_bytes=60 * 1024 * 1024
        ),
    )(*arrays)


def solution(mesh):
    in_specs = (
        P(("member", "face", "slot"), None),
        P(("member", "face", "slot"), None),
        P(("member", "face", "slot")),
        P(("face", "slot"), "chan"),
        P(None, ("face", "slot")),
        P(None, ("face", "slot")),
        P(),
        P(None, "chan"),
        P(None, "chan"),
        P("chan", None),
        P("chan", None),
    )
    out_specs = (P(("member", "face", "slot"), None), P(("member", "face", "slot"), "chan"))
    return jax.shard_map(body, mesh=mesh, in_specs=in_specs, out_specs=out_specs, check_vma=False)
```

```python
import functools

import jax
import jax.numpy as jnp
from jax import lax
from jax.experimental import pallas as pl
from jax.experimental.pallas import tpu as pltpu
from jax.sharding import PartitionSpec as P

HD = 64
HALO = 32
LANES = 128
INPUTS = 11
MESH = pl.DeviceIdType.MESH
F32 = jnp.float32
BF16 = jnp.bfloat16


def dot(a, b):
    return jnp.dot(a, b, preferred_element_type=F32)


def dot_tn(a, b):
    return lax.dot_general(a, b, (((0,), (0,)), ((), ())), preferred_element_type=F32)


def dot_nt(a, b):
    return lax.dot_general(a, b, (((1,), (1,)), ((), ())), preferred_element_type=F32)


def ones_where(mask):
    return jnp.where(mask, 1.0, 0.0).astype(BF16)


def two_parts(x):
    high = x.astype(BF16)
    return high, (x - high.astype(F32)).astype(BF16)


def kernel(
    faces,
    slots,
    *refs,
):
    arrays, refs = refs[:INPUTS], refs[INPUTS:]
    predicted, state_out = refs[:2]
    held, refs = refs[2 : 2 + INPUTS], refs[2 + INPUTS :]
    (
        load_sem,
        rows_out,
        rows_in,
        cells_out,
        cells_in,
        queries,
        embedded,
        numer,
        denom,
        sums_out,
        sums_in,
        ends,
        ends_out,
        ends_in,
        wide,
        mix_parts,
        back_out,
        back_in,
        part_out,
        part_in,
        table,
        chosen,
        row_sem,
        share_sem,
        cell_sem,
        query_sem,
        sums_sem,
        halo_sem,
        ends_sem,
        chan_sem,
        table_sem,
        core_sem,
    ) = refs
    loads = [
        pltpu.make_async_copy(array, into, load_sem.at[i])
        for i, (array, into) in enumerate(zip(arrays, held))
    ]
    for load in loads:
        load.start()
    (
        face_row,
        cell_row,
        observed,
        node_embed,
        w_embed,
        w_key,
        neighbours,
        edge_weight,
        w_mix,
        w_back,
        w_out,
    ) = held
    row_count = observed.shape[0]
    cap = rows_in.shape[1]
    nodes, width = node_embed.shape
    blocks = faces * slots
    face_nodes = slots * nodes
    face, slot, chan = lax.axis_index("face"), lax.axis_index("slot"), lax.axis_index("chan")
    block = face * slots + slot
    other = 1 - chan

    def block_id(index):
        return {"face": index // slots, "slot": lax.rem(index, slots)}

    barrier = pltpu.get_barrier_semaphore()

    def greet(k, carry):
        pl.semaphore_signal(
            barrier, inc=1, device_id=block_id(lax.rem(block + k, blocks)), device_id_type=MESH
        )
        return carry

    lax.fori_loop(1, blocks, greet, 0)
    pl.semaphore_signal(barrier, inc=1, device_id={"chan": other}, device_id_type=MESH)

    for load in loads[:4]:
        load.wait()

    face_of = face_row[...]
    sub = lax.broadcasted_iota(jnp.int32, (max(8, faces), row_count), 0)
    lane = lax.broadcasted_iota(jnp.int32, (max(8, faces), row_count), 1)
    aimed = jnp.where(sub == face_of, 1, 0)
    count = aimed
    step = 1
    while step < row_count:
        count = count + jnp.where(lane >= step, pltpu.roll(count, step, 1), 0)
        step *= 2
    place = jnp.sum(aimed * (count - 1), axis=0, keepdims=True) + face_of * cap
    cell1 = cell_row[...] + 1
    sub16 = lax.broadcasted_iota(jnp.int32, (16, row_count), 0)
    cell_parts = (
        jnp.where(sub16 == 0, cell1 >> 7, jnp.where(sub16 == 1, cell1 & 127, 0))
        .astype(F32)
        .astype(BF16)
    )

    def bucket(goal):
        pick = ones_where(
            lax.broadcasted_iota(jnp.int32, (cap, row_count), 0) == place - goal * cap
        )
        parts = dot_nt(cell_parts, pick)
        cells = (parts[0:1] * 128.0 + parts[1:2]).astype(jnp.int32) - 1
        return dot(pick, observed[...]).astype(BF16), cells

    def fill(k, carry):
        rows_out[k], cells_out[k] = bucket(lax.rem(face + k, faces))
        return carry

    rows_in[0], cells_in[0] = bucket(face)
    lax.fori_loop(1, faces, fill, 0)
    queries[pl.ds(slot * nodes, nodes)] = node_embed[...]

    pl.semaphore_wait(barrier, blocks)

    def query_copy(k):
        mine = queries.at[pl.ds(slot * nodes, nodes)]
        return pltpu.make_async_remote_copy(
            src_ref=node_embed,
            dst_ref=mine,
            send_sem=query_sem.at[0, k],
            recv_sem=query_sem.at[1, k],
            device_id={"slot": lax.rem(slot + k, slots)},
            device_id_type=MESH,
        )

    for k in range(1, slots):
        query_copy(k).start()

    share = cap // 2
    own_share = pl.ds(chan * share, share)

    def row_copy(k):
        return pltpu.make_async_remote_copy(
            src_ref=rows_out.at[k, own_share],
            dst_ref=rows_in.at[k, own_share],
            send_sem=row_sem.at[0, k],
            recv_sem=row_sem.at[1, k],
            device_id={"face": lax.rem(face + k, faces)},
            device_id_type=MESH,
        )

    def share_copy(k, core):
        rows = rows_in.at[k, pl.ds(core * share, share)]
        return pltpu.make_async_remote_copy(
            src_ref=rows,
            dst_ref=rows,
            send_sem=share_sem.at[0, k],
            recv_sem=share_sem.at[1, k],
            device_id={"chan": other},
            device_id_type=MESH,
        )

    def cell_copy(k):
        return pltpu.make_async_remote_copy(
            src_ref=cells_out.at[k],
            dst_ref=cells_in.at[k],
            send_sem=cell_sem.at[0, k],
            recv_sem=cell_sem.at[1, k],
            device_id={"face": lax.rem(face + k, faces)},
            device_id_type=MESH,
        )

    def send_rows(k, carry):
        row_copy(k).start()
        cell_copy(k).start()
        return carry

    lax.fori_loop(1, faces, send_rows, 0)

    def edge_copy(side, source, goal, sem):
        step = blocks - 1 if side == 0 else 1
        return pltpu.make_async_remote_copy(
            src_ref=source,
            dst_ref=goal,
            send_sem=halo_sem.at[0, sem],
            recv_sem=halo_sem.at[1, sem],
            device_id=block_id(lax.rem(block + step, blocks)),
            device_id_type=MESH,
        )

    to_left = edge_copy(0, node_embed.at[pl.ds(0, HALO)], ends.at[1], 0)
    to_right = edge_copy(1, node_embed.at[pl.ds(nodes - HALO, HALO)], ends.at[0], 1)
    to_left.start()
    to_right.start()

    group = ones_where(
        lax.broadcasted_iota(jnp.int32, (width, LANES), 0) // HD
        == lax.broadcasted_iota(jnp.int32, (width, LANES), 1)
    )
    spread = ones_where(
        lax.broadcasted_iota(jnp.int32, (LANES, width), 1) // HD
        == lax.broadcasted_iota(jnp.int32, (LANES, width), 0)
    )
    numer[...] = jnp.zeros_like(numer)
    denom[...] = jnp.zeros_like(denom)

    node_of = jnp.broadcast_to(face_of * face_nodes + cell_row[...], (LANES, row_count)).T
    lane_of = lax.broadcasted_iota(jnp.int32, (row_count, LANES), 1)
    piece = chosen.shape[1]

    def choose(first):
        for j in range(0, piece, LANES):
            chosen[:, j : j + LANES] = ones_where(lane_of == node_of - (first + j))

    if piece == blocks * nodes:
        choose(0)
    for load in loads[4:6]:
        load.wait()
    for k in range(1, slots):
        query_copy(k).wait()

    def attend_block(k, carry):
        @pl.when(k > 0)
        def _():
            cell_copy(k).wait()
            share_copy(k, other).wait_recv()

        x = rows_in[k]
        chunk = 256
        for j in range(0, w_embed.shape[1], chunk):
            embedded[:, j : j + chunk] = jax.nn.gelu(dot(x, w_embed[:, j : j + chunk])).astype(BF16)
        keys = dot(embedded[...], w_key[...]).astype(BF16).astype(F32)

        @pl.when(k + 1 < faces)
        def _():
            row_copy(k + 1).wait()
            share_copy(k + 1, chan).start()

        hit = ones_where(
            lax.broadcasted_iota(jnp.int32, (face_nodes, cap), 0) == cells_in[k][0:1]
        )
        picked = dot_tn(hit, queries[...])
        score = dot((picked * keys).astype(BF16), group) * (HD**-0.5)
        attend = jax.nn.sigmoid(score).astype(BF16)
        values = embedded[:, pl.ds(pl.multiple_of(chan * width, width), width)]
        contrib = (dot(attend, spread) * values.astype(F32)).astype(BF16)
        numer[...] += dot(hit, contrib)
        denom[...] += dot(hit, attend)
        return carry

    lax.fori_loop(0, faces, attend_block, 0)

    def finish_share(k, carry):
        share_copy(k, chan).wait_send()
        return carry

    lax.fori_loop(1, faces, finish_share, 0)

    def sums_copy(k):
        return pltpu.make_async_remote_copy(
            src_ref=sums_out.at[k],
            dst_ref=sums_in.at[k],
            send_sem=sums_sem.at[0, k],
            recv_sem=sums_sem.at[1, k],
            device_id={"slot": lax.rem(slot + k, slots)},
            device_id_type=MESH,
        )

    def end_goal(side, k):
        return lax.rem(face * slots + k + (1 if side == 0 else blocks - 1), blocks)

    def end_source(side, k):
        step = blocks - 1 if side == 0 else 1
        return lax.rem(block + step, blocks) // slots * slots + k

    def end_copy(side, k, source_slot):
        return pltpu.make_async_remote_copy(
            src_ref=ends_out.at[side, k],
            dst_ref=ends_in.at[side, slot],
            send_sem=ends_sem.at[0, side, k],
            recv_sem=ends_sem.at[1, side, source_slot],
            device_id=block_id(end_goal(side, k)),
            device_id_type=MESH,
        )

    def end_arrival(side, k):
        return pltpu.make_async_remote_copy(
            src_ref=ends_out.at[side, k],
            dst_ref=ends_in.at[side, k],
            send_sem=ends_sem.at[0, side, k],
            recv_sem=ends_sem.at[1, side, k],
            device_id=block_id(end_goal(side, k)),
            device_id_type=MESH,
        )

    for side in range(2):
        for k in range(slots):
            edge = pl.ds(k * nodes + (nodes - HALO if side == 0 else 0), HALO)
            sums = numer[edge].astype(BF16)
            counts = denom[edge].astype(BF16)
            away = end_goal(side, k) != block

            @pl.when(away)
            def _():
                ends_out[side, k, :, :width] = sums
                ends_out[side, k, :, width:] = counts
                end_copy(side, k, slot).start()

            @pl.when(jnp.logical_not(away))
            def _():
                ends_in[side, slot, :, :width] = sums
                ends_in[side, slot, :, width:] = counts

    for k in range(1, slots):
        theirs = pl.ds(lax.rem(slot + k, slots) * nodes, nodes)
        sums_out[k, :, :width] = numer[theirs].astype(BF16)
        sums_out[k, :, width:] = denom[theirs].astype(BF16)
        sums_copy(k).start()

    for load in loads[6:]:
        load.wait()

    extended = nodes + 2 * HALO
    position = lax.broadcasted_iota(jnp.int32, (extended, nodes), 0)
    weights = jnp.zeros((extended, nodes), F32)
    for j in range(neighbours.shape[0]):
        weights += jnp.where(position == neighbours[j : j + 1], edge_weight[j : j + 1], 0.0)
    weights_high, weights_low = two_parts(weights)

    mine = pl.ds(slot * nodes, nodes)
    total = numer[mine]
    weight = denom[mine]
    for k in range(1, slots):
        sums_copy(k).wait()
        total += sums_in[k, :, :width].astype(F32)
        weight += sums_in[k, :, width:].astype(F32)

    def latent_of(features, total, weight):
        high, low = two_parts(weight)
        weight = dot(high, spread) + dot(low, spread)
        return (features.astype(F32) + total / (1.0 + weight)).astype(BF16)

    latent = latent_of(node_embed[...], total, weight)
    wide[HALO : HALO + nodes] = latent
    to_left.wait()
    to_right.wait()
    for side in range(2):
        for k in range(slots):

            @pl.when(end_goal(side, k) != block)
            def _():
                end_copy(side, k, slot).wait_send()

            @pl.when(end_source(side, k) != block)
            def _():
                end_arrival(side, k).wait_recv()

        both = ends_in[side, 0].astype(F32)
        for k in range(1, slots):
            both += ends_in[side, k].astype(F32)
        first = 0 if side == 0 else HALO + nodes
        wide[first : first + HALO] = latent_of(ends[side], both[:, :width], both[:, width:])

    def chan_copy(k, source, goal):
        return pltpu.make_async_remote_copy(
            src_ref=source,
            dst_ref=goal,
            send_sem=chan_sem.at[0, k],
            recv_sem=chan_sem.at[1, k],
            device_id={"chan": other},
            device_id_type=MESH,
        )

    around = wide[...]
    summed = (dot_tn(weights_high, around) + dot_tn(weights_low, around)).astype(BF16)
    mix_parts[0] = summed
    mix_copy = chan_copy(0, mix_parts.at[0], mix_parts.at[1])
    mix_copy.start()
    mixed = dot(summed, w_mix[pl.ds(pl.multiple_of(chan * width, width), width)])
    mix_copy.wait()
    mixed += dot(mix_parts[1], w_mix[pl.ds(pl.multiple_of(other * width, width), width)])
    hidden = jax.nn.gelu(mixed).astype(BF16)
    back_out[...] = dot(
        hidden, w_back[:, pl.ds(pl.multiple_of(other * width, width), width)]
    ).astype(BF16)
    back_copy = chan_copy(1, back_out, back_in)
    back_copy.start()
    update = dot(hidden, w_back[:, pl.ds(pl.multiple_of(chan * width, width), width)])
    back_copy.wait()
    state = (latent.astype(F32) + update + back_in[...].astype(F32)).astype(BF16)
    state_out[...] = state

    part = dot(state, w_out[...])
    part_out[...] = part
    half = nodes // 2
    part_copy = chan_copy(2, part_out.at[pl.ds(other * half, half)], part_in)
    part_copy.start()
    part_copy.wait()
    part = part_out[pl.ds(chan * half, half)] + part_in[...]
    table[pl.ds(block * nodes + chan * half, half)] = part.astype(BF16)

    def half_copy(k, place, core, sems, goal):
        source = lax.rem(block + blocks - place, blocks)
        rows = table.at[pl.ds(source * nodes + core * half, half)]
        return pltpu.make_async_remote_copy(
            src_ref=rows,
            dst_ref=rows,
            send_sem=sems.at[0, k],
            recv_sem=sems.at[1, k],
            device_id=goal,
            device_id_type=MESH,
        )

    def to_block(k, place):
        goal = block_id(lax.rem(block + k, blocks))
        return half_copy(k, place, chan, table_sem, goal)

    def to_chan(k, core):
        return half_copy(k, k, core, core_sem, {"chan": other})

    def start_block(k, carry):
        to_block(k, 0).start()
        return carry

    def forward(k, carry):
        to_block(k, k).wait_recv()
        to_chan(k, chan).start()
        return carry

    def finish(k, carry):
        @pl.when(k > 0)
        def _():
            to_block(k, 0).wait_send()

        to_chan(k, chan).wait_send()
        to_chan(k, other).wait_recv()
        return carry

    lax.fori_loop(1, blocks, start_block, 0)
    to_chan(0, chan).start()
    lax.fori_loop(1, blocks, forward, 0)
    lax.fori_loop(0, blocks, finish, 0)
    if piece == blocks * nodes:
        total = dot(chosen[...], table[...])
    else:

        def decode(k, total):
            choose(k * piece)
            return total + dot(chosen[...], table[pl.ds(k * piece, piece)])

        total = jnp.zeros(predicted.shape, F32)
        total = lax.fori_loop(0, blocks * nodes // piece, decode, total)
    predicted[...] = total.astype(BF16)


def body(
    observed,
    target_face,
    target_cell,
    node_embed,
    neighbours,
    edge_weight,
    w_embed,
    w_key,
    w_mix,
    w_back,
    w_out,
):
    faces, slots = lax.axis_size("face"), lax.axis_size("slot")
    row_count, features = observed.shape
    nodes, width = node_embed.shape
    channels = w_embed.shape[1]
    cap = 2 * row_count // faces
    blocks = faces * slots
    face_row = target_face.reshape(1, row_count)
    cell_row = target_cell.reshape(1, row_count)
    piece = blocks * nodes if blocks * nodes <= 4096 else slots * nodes
    arrays = (
        face_row,
        cell_row,
        observed,
        node_embed,
        w_embed,
        w_key,
        neighbours,
        edge_weight,
        w_mix,
        w_back,
        w_out,
    )
    vmem = pl.BlockSpec(memory_space=pltpu.VMEM)
    dma = pltpu.SemaphoreType.DMA
    return pl.pallas_call(
        functools.partial(kernel, faces, slots),
        out_shape=(
            jax.ShapeDtypeStruct((row_count, w_out.shape[1]), BF16),
            jax.ShapeDtypeStruct((nodes, width), BF16),
        ),
        in_specs=[pl.BlockSpec(memory_space=pl.ANY)] * INPUTS,
        out_specs=(vmem, vmem),
        scratch_shapes=[pltpu.VMEM(array.shape, array.dtype) for array in arrays]
        + [
            dma((INPUTS,)),
            pltpu.VMEM((faces, cap, features), BF16),
            pltpu.VMEM((faces, cap, features), BF16),
            pltpu.VMEM((faces, 1, cap), jnp.int32),
            pltpu.VMEM((faces, 1, cap), jnp.int32),
            pltpu.VMEM((slots * nodes, width), BF16),
            pltpu.VMEM((cap, channels), BF16),
            pltpu.VMEM((slots * nodes, width), F32),
            pltpu.VMEM((slots * nodes, LANES), F32),
            pltpu.VMEM((slots, nodes, width + LANES), BF16),
            pltpu.VMEM((slots, nodes, width + LANES), BF16),
            pltpu.VMEM((2, HALO, width), BF16),
            pltpu.VMEM((2, slots, HALO, width + LANES), BF16),
            pltpu.VMEM((2, slots, HALO, width + LANES), BF16),
            pltpu.VMEM((nodes + 2 * HALO, width), BF16),
            pltpu.VMEM((2, nodes, width), BF16),
            pltpu.VMEM((nodes, width), BF16),
            pltpu.VMEM((nodes, width), BF16),
            pltpu.VMEM((nodes, w_out.shape[1]), F32),
            pltpu.VMEM((nodes // 2, w_out.shape[1]), F32),
            pltpu.VMEM((blocks * nodes, w_out.shape[1]), BF16),
            pltpu.VMEM((row_count, piece), BF16),
            dma((2, faces)),
            dma((2, faces)),
            dma((2, faces)),
            dma((2, slots)),
            dma((2, slots)),
            dma((2, 2)),
            dma((2, 2, slots)),
            dma((2, 3)),
            dma((2, blocks)),
            dma((2, blocks)),
        ],
        compiler_params=pltpu.CompilerParams(
            collective_id=0, has_side_effects=True, vmem_limit_bytes=60 * 1024 * 1024
        ),
    )(*arrays)


def solution(mesh):
    in_specs = (
        P(("member", "face", "slot"), None),
        P(("member", "face", "slot"), None),
        P(("member", "face", "slot")),
        P(("face", "slot"), "chan"),
        P(None, ("face", "slot")),
        P(None, ("face", "slot")),
        P(),
        P(None, "chan"),
        P(None, "chan"),
        P("chan", None),
        P("chan", None),
    )
    out_specs = (P(("member", "face", "slot"), None), P(("member", "face", "slot"), "chan"))
    return jax.shard_map(body, mesh=mesh, in_specs=in_specs, out_specs=out_specs, check_vma=False)
```

```python
import functools

import jax
import jax.numpy as jnp
from jax import lax
from jax.experimental import pallas as pl
from jax.experimental.pallas import tpu as pltpu
from jax.sharding import PartitionSpec as P

HD = 64
HALO = 32
LANES = 128
INPUTS = 11
MESH = pl.DeviceIdType.MESH
F32 = jnp.float32
BF16 = jnp.bfloat16


def dot(a, b):
    return jnp.dot(a, b, preferred_element_type=F32)


def dot_tn(a, b):
    return lax.dot_general(a, b, (((0,), (0,)), ((), ())), preferred_element_type=F32)


def dot_nt(a, b):
    return lax.dot_general(a, b, (((1,), (1,)), ((), ())), preferred_element_type=F32)


def ones_where(mask):
    return jnp.where(mask, 1.0, 0.0).astype(BF16)


def two_parts(x):
    high = x.astype(BF16)
    return high, (x - high.astype(F32)).astype(BF16)


def kernel(
    faces,
    slots,
    *refs,
):
    arrays, refs = refs[:INPUTS], refs[INPUTS:]
    predicted, state_out = refs[:2]
    held, refs = refs[2 : 2 + INPUTS], refs[2 + INPUTS :]
    (
        load_sem,
        rows_out,
        rows_in,
        cells_out,
        cells_in,
        queries,
        embedded,
        numer,
        denom,
        sums_out,
        sums_in,
        ends,
        ends_out,
        ends_in,
        wide,
        mix_parts,
        back_out,
        back_in,
        part_out,
        part_in,
        table,
        chosen,
        row_sem,
        share_sem,
        cell_sem,
        query_sem,
        sums_sem,
        halo_sem,
        ends_sem,
        chan_sem,
        table_sem,
        core_sem,
    ) = refs
    loads = [
        pltpu.make_async_copy(array, into, load_sem.at[i])
        for i, (array, into) in enumerate(zip(arrays, held))
    ]
    for load in loads:
        load.start()
    (
        face_row,
        cell_row,
        observed,
        node_embed,
        w_embed,
        w_key,
        neighbours,
        edge_weight,
        w_mix,
        w_back,
        w_out,
    ) = held
    row_count = observed.shape[0]
    cap = rows_in.shape[1]
    nodes, width = node_embed.shape
    blocks = faces * slots
    face_nodes = slots * nodes
    face, slot, chan = lax.axis_index("face"), lax.axis_index("slot"), lax.axis_index("chan")
    block = face * slots + slot
    other = 1 - chan

    def block_id(index):
        return {"face": index // slots, "slot": lax.rem(index, slots)}

    barrier = pltpu.get_barrier_semaphore()

    def greet(k, carry):
        pl.semaphore_signal(
            barrier, inc=1, device_id=block_id(lax.rem(block + k, blocks)), device_id_type=MESH
        )
        return carry

    lax.fori_loop(1, blocks, greet, 0)
    pl.semaphore_signal(barrier, inc=1, device_id={"chan": other}, device_id_type=MESH)

    for load in loads[:4]:
        load.wait()

    face_of = face_row[...]
    sub = lax.broadcasted_iota(jnp.int32, (max(8, faces), row_count), 0)
    lane = lax.broadcasted_iota(jnp.int32, (max(8, faces), row_count), 1)
    aimed = jnp.where(sub == face_of, 1, 0)
    count = aimed
    step = 1
    while step < row_count:
        count = count + jnp.where(lane >= step, pltpu.roll(count, step, 1), 0)
        step *= 2
    place = jnp.sum(aimed * (count - 1), axis=0, keepdims=True) + face_of * cap
    cell1 = cell_row[...] + 1
    sub16 = lax.broadcasted_iota(jnp.int32, (16, row_count), 0)
    cell_parts = (
        jnp.where(sub16 == 0, cell1 >> 7, jnp.where(sub16 == 1, cell1 & 127, 0))
        .astype(F32)
        .astype(BF16)
    )

    def bucket(goal):
        pick = ones_where(
            lax.broadcasted_iota(jnp.int32, (cap, row_count), 0) == place - goal * cap
        )
        parts = dot_nt(cell_parts, pick)
        cells = (parts[0:1] * 128.0 + parts[1:2]).astype(jnp.int32) - 1
        return dot(pick, observed[...]).astype(BF16), cells

    def fill(k, carry):
        rows_out[k], cells_out[k] = bucket(lax.rem(face + k, faces))
        return carry

    rows_in[0], cells_in[0] = bucket(face)
    lax.fori_loop(1, faces, fill, 0)
    queries[pl.ds(slot * nodes, nodes)] = node_embed[...]

    pl.semaphore_wait(barrier, blocks)

    def query_copy(k):
        mine = queries.at[pl.ds(slot * nodes, nodes)]
        return pltpu.make_async_remote_copy(
            src_ref=node_embed,
            dst_ref=mine,
            send_sem=query_sem.at[0, k],
            recv_sem=query_sem.at[1, k],
            device_id={"slot": lax.rem(slot + k, slots)},
            device_id_type=MESH,
        )

    for k in range(1, slots):
        query_copy(k).start()

    share = cap // 2
    own_share = pl.ds(chan * share, share)

    def row_copy(k):
        return pltpu.make_async_remote_copy(
            src_ref=rows_out.at[k, own_share],
            dst_ref=rows_in.at[k, own_share],
            send_sem=row_sem.at[0, k],
            recv_sem=row_sem.at[1, k],
            device_id={"face": lax.rem(face + k, faces)},
            device_id_type=MESH,
        )

    def share_copy(k, core):
        rows = rows_in.at[k, pl.ds(core * share, share)]
        return pltpu.make_async_remote_copy(
            src_ref=rows,
            dst_ref=rows,
            send_sem=share_sem.at[0, k],
            recv_sem=share_sem.at[1, k],
            device_id={"chan": other},
            device_id_type=MESH,
        )

    def cell_copy(k):
        return pltpu.make_async_remote_copy(
            src_ref=cells_out.at[k],
            dst_ref=cells_in.at[k],
            send_sem=cell_sem.at[0, k],
            recv_sem=cell_sem.at[1, k],
            device_id={"face": lax.rem(face + k, faces)},
            device_id_type=MESH,
        )

    def send_rows(k, carry):
        row_copy(k).start()
        cell_copy(k).start()
        return carry

    lax.fori_loop(1, faces, send_rows, 0)

    def edge_copy(side, source, goal, sem):
        step = blocks - 1 if side == 0 else 1
        return pltpu.make_async_remote_copy(
            src_ref=source,
            dst_ref=goal,
            send_sem=halo_sem.at[0, sem],
            recv_sem=halo_sem.at[1, sem],
            device_id=block_id(lax.rem(block + step, blocks)),
            device_id_type=MESH,
        )

    to_left = edge_copy(0, node_embed.at[pl.ds(0, HALO)], ends.at[1], 0)
    to_right = edge_copy(1, node_embed.at[pl.ds(nodes - HALO, HALO)], ends.at[0], 1)
    to_left.start()
    to_right.start()

    group = ones_where(
        lax.broadcasted_iota(jnp.int32, (width, LANES), 0) // HD
        == lax.broadcasted_iota(jnp.int32, (width, LANES), 1)
    )
    spread = ones_where(
        lax.broadcasted_iota(jnp.int32, (LANES, width), 1) // HD
        == lax.broadcasted_iota(jnp.int32, (LANES, width), 0)
    )
    numer[...] = jnp.zeros_like(numer)
    denom[...] = jnp.zeros_like(denom)

    node_of = jnp.broadcast_to(face_of * face_nodes + cell_row[...], (LANES, row_count)).T
    lane_of = lax.broadcasted_iota(jnp.int32, (row_count, LANES), 1)
    piece = chosen.shape[1]

    def choose(first):
        for j in range(0, piece, LANES):
            chosen[:, j : j + LANES] = ones_where(lane_of == node_of - (first + j))

    for load in loads[4:6]:
        load.wait()
    for k in range(1, slots):
        query_copy(k).wait()

    def attend_block(k, carry):
        @pl.when(k > 0)
        def _():
            cell_copy(k).wait()
            share_copy(k, other).wait_recv()

        x = rows_in[k]
        chunk = 256
        for j in range(0, w_embed.shape[1], chunk):
            embedded[:, j : j + chunk] = jax.nn.gelu(dot(x, w_embed[:, j : j + chunk])).astype(BF16)
        keys = dot(embedded[...], w_key[...]).astype(BF16).astype(F32)

        @pl.when(k + 1 < faces)
        def _():
            row_copy(k + 1).wait()
            share_copy(k + 1, chan).start()

        hit = ones_where(
            lax.broadcasted_iota(jnp.int32, (face_nodes, cap), 0) == cells_in[k][0:1]
        )
        picked = dot_tn(hit, queries[...])
        score = dot((picked * keys).astype(BF16), group) * (HD**-0.5)
        attend = jax.nn.sigmoid(score).astype(BF16)
        values = embedded[:, pl.ds(pl.multiple_of(chan * width, width), width)]
        contrib = (dot(attend, spread) * values.astype(F32)).astype(BF16)
        numer[...] += dot(hit, contrib)
        denom[...] += dot(hit, attend)
        return carry

    lax.fori_loop(0, faces, attend_block, 0)

    def finish_share(k, carry):
        share_copy(k, chan).wait_send()
        return carry

    lax.fori_loop(1, faces, finish_share, 0)

    def sums_copy(k):
        return pltpu.make_async_remote_copy(
            src_ref=sums_out.at[k],
            dst_ref=sums_in.at[k],
            send_sem=sums_sem.at[0, k],
            recv_sem=sums_sem.at[1, k],
            device_id={"slot": lax.rem(slot + k, slots)},
            device_id_type=MESH,
        )

    def end_goal(side, k):
        return lax.rem(face * slots + k + (1 if side == 0 else blocks - 1), blocks)

    def end_source(side, k):
        step = blocks - 1 if side == 0 else 1
        return lax.rem(block + step, blocks) // slots * slots + k

    def end_copy(side, k, source_slot):
        return pltpu.make_async_remote_copy(
            src_ref=ends_out.at[side, k],
            dst_ref=ends_in.at[side, slot],
            send_sem=ends_sem.at[0, side, k],
            recv_sem=ends_sem.at[1, side, source_slot],
            device_id=block_id(end_goal(side, k)),
            device_id_type=MESH,
        )

    def end_arrival(side, k):
        return pltpu.make_async_remote_copy(
            src_ref=ends_out.at[side, k],
            dst_ref=ends_in.at[side, k],
            send_sem=ends_sem.at[0, side, k],
            recv_sem=ends_sem.at[1, side, k],
            device_id=block_id(end_goal(side, k)),
            device_id_type=MESH,
        )

    for side in range(2):
        for k in range(slots):
            edge = pl.ds(k * nodes + (nodes - HALO if side == 0 else 0), HALO)
            sums = numer[edge].astype(BF16)
            counts = denom[edge].astype(BF16)
            away = end_goal(side, k) != block

            @pl.when(away)
            def _():
                ends_out[side, k, :, :width] = sums
                ends_out[side, k, :, width:] = counts
                end_copy(side, k, slot).start()

            @pl.when(jnp.logical_not(away))
            def _():
                ends_in[side, slot, :, :width] = sums
                ends_in[side, slot, :, width:] = counts

    for k in range(1, slots):
        theirs = pl.ds(lax.rem(slot + k, slots) * nodes, nodes)
        sums_out[k, :, :width] = numer[theirs].astype(BF16)
        sums_out[k, :, width:] = denom[theirs].astype(BF16)
        sums_copy(k).start()

    for load in loads[6:]:
        load.wait()

    extended = nodes + 2 * HALO
    position = lax.broadcasted_iota(jnp.int32, (extended, nodes), 0)
    weights = jnp.zeros((extended, nodes), F32)
    for j in range(neighbours.shape[0]):
        weights += jnp.where(position == neighbours[j : j + 1], edge_weight[j : j + 1], 0.0)
    weights_high, weights_low = two_parts(weights)

    if piece == blocks * nodes:
        choose(0)
    mine = pl.ds(slot * nodes, nodes)
    total = numer[mine]
    weight = denom[mine]
    for k in range(1, slots):
        sums_copy(k).wait()
        total += sums_in[k, :, :width].astype(F32)
        weight += sums_in[k, :, width:].astype(F32)

    def latent_of(features, total, weight):
        high, low = two_parts(weight)
        weight = dot(high, spread) + dot(low, spread)
        return (features.astype(F32) + total / (1.0 + weight)).astype(BF16)

    latent = latent_of(node_embed[...], total, weight)
    wide[HALO : HALO + nodes] = latent
    to_left.wait()
    to_right.wait()
    for side in range(2):
        for k in range(slots):

            @pl.when(end_goal(side, k) != block)
            def _():
                end_copy(side, k, slot).wait_send()

            @pl.when(end_source(side, k) != block)
            def _():
                end_arrival(side, k).wait_recv()

        both = ends_in[side, 0].astype(F32)
        for k in range(1, slots):
            both += ends_in[side, k].astype(F32)
        first = 0 if side == 0 else HALO + nodes
        wide[first : first + HALO] = latent_of(ends[side], both[:, :width], both[:, width:])

    def chan_copy(k, source, goal):
        return pltpu.make_async_remote_copy(
            src_ref=source,
            dst_ref=goal,
            send_sem=chan_sem.at[0, k],
            recv_sem=chan_sem.at[1, k],
            device_id={"chan": other},
            device_id_type=MESH,
        )

    around = wide[...]
    summed = (dot_tn(weights_high, around) + dot_tn(weights_low, around)).astype(BF16)
    mix_parts[0] = summed
    mix_copy = chan_copy(0, mix_parts.at[0], mix_parts.at[1])
    mix_copy.start()
    mixed = dot(summed, w_mix[pl.ds(pl.multiple_of(chan * width, width), width)])
    mix_copy.wait()
    mixed += dot(mix_parts[1], w_mix[pl.ds(pl.multiple_of(other * width, width), width)])
    hidden = jax.nn.gelu(mixed).astype(BF16)
    back_out[...] = dot(
        hidden, w_back[:, pl.ds(pl.multiple_of(other * width, width), width)]
    ).astype(BF16)
    back_copy = chan_copy(1, back_out, back_in)
    back_copy.start()
    update = dot(hidden, w_back[:, pl.ds(pl.multiple_of(chan * width, width), width)])
    back_copy.wait()
    state = (latent.astype(F32) + update + back_in[...].astype(F32)).astype(BF16)
    state_out[...] = state

    part = dot(state, w_out[...])
    part_out[...] = part
    half = nodes // 2
    part_copy = chan_copy(2, part_out.at[pl.ds(other * half, half)], part_in)
    part_copy.start()
    part_copy.wait()
    part = part_out[pl.ds(chan * half, half)] + part_in[...]
    table[pl.ds(block * nodes + chan * half, half)] = part.astype(BF16)

    def half_copy(k, place, core, sems, goal):
        source = lax.rem(block + blocks - place, blocks)
        rows = table.at[pl.ds(source * nodes + core * half, half)]
        return pltpu.make_async_remote_copy(
            src_ref=rows,
            dst_ref=rows,
            send_sem=sems.at[0, k],
            recv_sem=sems.at[1, k],
            device_id=goal,
            device_id_type=MESH,
        )

    def to_block(k, place):
        goal = block_id(lax.rem(block + k, blocks))
        return half_copy(k, place, chan, table_sem, goal)

    def to_chan(k, core):
        return half_copy(k, k, core, core_sem, {"chan": other})

    def start_block(k, carry):
        to_block(k, 0).start()
        return carry

    def forward(k, carry):
        to_block(k, k).wait_recv()
        to_chan(k, chan).start()
        return carry

    def finish(k, carry):
        @pl.when(k > 0)
        def _():
            to_block(k, 0).wait_send()

        to_chan(k, chan).wait_send()
        to_chan(k, other).wait_recv()
        return carry

    lax.fori_loop(1, blocks, start_block, 0)
    to_chan(0, chan).start()
    lax.fori_loop(1, blocks, forward, 0)
    lax.fori_loop(0, blocks, finish, 0)
    if piece == blocks * nodes:
        total = dot(chosen[...], table[...])
    else:

        def decode(k, total):
            choose(k * piece)
            return total + dot(chosen[...], table[pl.ds(k * piece, piece)])

        total = jnp.zeros(predicted.shape, F32)
        total = lax.fori_loop(0, blocks * nodes // piece, decode, total)
    predicted[...] = total.astype(BF16)


def body(
    observed,
    target_face,
    target_cell,
    node_embed,
    neighbours,
    edge_weight,
    w_embed,
    w_key,
    w_mix,
    w_back,
    w_out,
):
    faces, slots = lax.axis_size("face"), lax.axis_size("slot")
    row_count, features = observed.shape
    nodes, width = node_embed.shape
    channels = w_embed.shape[1]
    cap = 2 * row_count // faces
    blocks = faces * slots
    face_row = target_face.reshape(1, row_count)
    cell_row = target_cell.reshape(1, row_count)
    piece = blocks * nodes if blocks * nodes <= 4096 else slots * nodes
    arrays = (
        face_row,
        cell_row,
        observed,
        node_embed,
        w_embed,
        w_key,
        neighbours,
        edge_weight,
        w_mix,
        w_back,
        w_out,
    )
    vmem = pl.BlockSpec(memory_space=pltpu.VMEM)
    dma = pltpu.SemaphoreType.DMA
    return pl.pallas_call(
        functools.partial(kernel, faces, slots),
        out_shape=(
            jax.ShapeDtypeStruct((row_count, w_out.shape[1]), BF16),
            jax.ShapeDtypeStruct((nodes, width), BF16),
        ),
        in_specs=[pl.BlockSpec(memory_space=pl.ANY)] * INPUTS,
        out_specs=(vmem, vmem),
        scratch_shapes=[pltpu.VMEM(array.shape, array.dtype) for array in arrays]
        + [
            dma((INPUTS,)),
            pltpu.VMEM((faces, cap, features), BF16),
            pltpu.VMEM((faces, cap, features), BF16),
            pltpu.VMEM((faces, 1, cap), jnp.int32),
            pltpu.VMEM((faces, 1, cap), jnp.int32),
            pltpu.VMEM((slots * nodes, width), BF16),
            pltpu.VMEM((cap, channels), BF16),
            pltpu.VMEM((slots * nodes, width), F32),
            pltpu.VMEM((slots * nodes, LANES), F32),
            pltpu.VMEM((slots, nodes, width + LANES), BF16),
            pltpu.VMEM((slots, nodes, width + LANES), BF16),
            pltpu.VMEM((2, HALO, width), BF16),
            pltpu.VMEM((2, slots, HALO, width + LANES), BF16),
            pltpu.VMEM((2, slots, HALO, width + LANES), BF16),
            pltpu.VMEM((nodes + 2 * HALO, width), BF16),
            pltpu.VMEM((2, nodes, width), BF16),
            pltpu.VMEM((nodes, width), BF16),
            pltpu.VMEM((nodes, width), BF16),
            pltpu.VMEM((nodes, w_out.shape[1]), F32),
            pltpu.VMEM((nodes // 2, w_out.shape[1]), F32),
            pltpu.VMEM((blocks * nodes, w_out.shape[1]), BF16),
            pltpu.VMEM((row_count, piece), BF16),
            dma((2, faces)),
            dma((2, faces)),
            dma((2, faces)),
            dma((2, slots)),
            dma((2, slots)),
            dma((2, 2)),
            dma((2, 2, slots)),
            dma((2, 3)),
            dma((2, blocks)),
            dma((2, blocks)),
        ],
        compiler_params=pltpu.CompilerParams(
            collective_id=0, has_side_effects=True, vmem_limit_bytes=60 * 1024 * 1024
        ),
    )(*arrays)


def solution(mesh):
    in_specs = (
        P(("member", "face", "slot"), None),
        P(("member", "face", "slot"), None),
        P(("member", "face", "slot")),
        P(("face", "slot"), "chan"),
        P(None, ("face", "slot")),
        P(None, ("face", "slot")),
        P(),
        P(None, "chan"),
        P(None, "chan"),
        P("chan", None),
        P("chan", None),
    )
    out_specs = (P(("member", "face", "slot"), None), P(("member", "face", "slot"), "chan"))
    return jax.shard_map(body, mesh=mesh, in_specs=in_specs, out_specs=out_specs, check_vma=False)
```
